32 devices in a mesh: groups: 2 (over x), tm: 2 (over core), slab: 8 (over z, y).
Axes of the slice: x: 2, y: 2, z: 4, core: 2. Of those that a mesh axis runs over, the one named last changes fastest.
Arguments:
- window_states: float32 [8, 64, 16, 512], P('tm', ('groups', 'slab')), parts along dimension 1, may hold values from -6 to 6
- spatial_weight: bfloat16 [320, 144], replicated, may hold values from -0.5 to 0.5
- temporal_weight: bfloat16 [3, 320, 320], replicated, may hold values from -0.1875 to 0.1875
- out_weight: bfloat16 [16, 320], replicated, may hold values from -0.3125 to 0.3125
- time_embed: float32 [1000, 320], replicated, may hold values from -6 to 6
- step_size: float32 [1000], replicated, may hold values from 0.1 to 0.4
- time_index: int32 [48], P('groups'), parts along dimension 0, may hold values from 0 to 999
- slides: int32 [4], P('groups'), parts along dimension 0, may hold values from 1 to 7
Outputs:
- final_states: float32 [8, 64, 16, 512], P('tm', ('groups', 'slab')), parts along dimension 1
The draws below stay inside these ranges and needn't reach their ends.
There are 2 independent parts, one for each index of `groups`. The reference program is written for one: setup_inputs(seed, part) draws one part's arguments, and reference() takes and returns one part's arrays. A program takes and returns all parts, laid end to end along the dimension named above; an argument that names none is the same for every part. Nothing has to cross between parts.
All inputs are finite; a program needn't handle non-finite values.
Results may differ from the reference program's by a relative error of at most 0.002.
Values may be sent and summed in bfloat16 or wider, within the bound.
A program may use at most 128 MiB of HBM per device.

```python
import math
import jax
import jax.numpy as jnp
from jax import lax

C = 16
HID = 320
HEIGHT = 16
WIDTH = 32
NSTEPS = 1000
WIN = 8
ITERS = 2
FRAMES = 32
HORIZON = 24


def set_ends(array, key, low, high):
    shape = array.shape
    spot = [jax.random.randint(jax.random.fold_in(key, axis), (), 0, shape[axis]) for axis in range(len(shape))]
    array = array.at[tuple(spot)].set(low)
    longest = shape.index(max(shape))
    spot[longest] = (spot[longest] + 1) % shape[longest]
    return array.at[tuple(spot)].set(high)


def block_scale(own_key, shape, split, least, largest):
    gain = 1.0
    for position, blocks in split:
        draws = jax.random.uniform(jax.random.fold_in(jax.random.fold_in(own_key, 6), position), (blocks,), jnp.float32, least / len(split), largest / len(split))
        gain = gain * jnp.repeat(jnp.exp(draws), shape[position] // blocks).reshape((-1,) + (1,) * (len(shape) - 1 - position))
    return gain


def gaussian(own_key, shape, width, bound, cuts=(), held_as=jnp.bfloat16):
    factor_of = block_scale(own_key, shape, cuts, -0.22, 0.18) if cuts else 1.0
    entries = jax.random.normal(own_key, shape, jnp.float32) * width * factor_of
    return jnp.minimum(jnp.maximum(entries, -bound), bound).astype(held_as)


def setup_inputs(seed: int = 0, part: int = 0) -> dict:
    key_list = jax.random.split(jax.random.key(seed), 9)
    part_splits = jax.random.split(jax.random.fold_in(key_list[8], part), 9)
    window_states = gaussian(part_splits[0], (WIN, FRAMES, C, HEIGHT * WIDTH), 1.0, 6.0, ((0, 2), (1, 8)), jnp.float32)
    spatial_weight = gaussian(key_list[1], (HID, 9 * C), (9 * C) ** -0.5, 0.5)
    temporal_weight = gaussian(key_list[2], (3, HID, HID), (3 * HID) ** -0.5, 0.1875)
    out_weight = gaussian(key_list[3], (C, HID), HID ** -0.5, 0.3125)
    time_embed = gaussian(key_list[4], (NSTEPS, HID), 1.0, 6.0, (), jnp.float32)
    step_size = jnp.clip(jnp.exp(jax.random.uniform(key_list[5], (NSTEPS,), jnp.float32, math.log(0.1), math.log(0.4))), 0.1, 0.4)
    time_index = set_ends(jax.random.randint(part_splits[6], (HORIZON,), 0, NSTEPS), jax.random.fold_in(part_splits[6], 1), 0, NSTEPS - 1).astype(jnp.int32)
    slides = jax.random.randint(part_splits[7], (ITERS,), 1, WIN).astype(jnp.int32)
    return {"window_states": window_states, "spatial_weight": spatial_weight, "temporal_weight": temporal_weight, "out_weight": out_weight, "time_embed": time_embed, "step_size": step_size, "time_index": time_index, "slides": slides}


def drift_one(item, spatial_weight, temporal_weight, out_weight):
    states_one, embed_one = item
    latent = states_one.astype(jnp.bfloat16).reshape(FRAMES, C, HEIGHT, WIDTH)
    padded = jnp.pad(latent, ((0, 0), (0, 0), (1, 1), (1, 1)))
    pieces = []
    for row_shift in range(3):
        for col_shift in range(3):
            pieces.append(padded[:, :, row_shift:row_shift + HEIGHT, col_shift:col_shift + WIDTH])
    columns = jnp.concatenate(pieces, axis=1).reshape(FRAMES, 9 * C, HEIGHT * WIDTH)
    pre = jnp.einsum("oc,fcp->fop", spatial_weight.astype(jnp.float32), columns.astype(jnp.float32))
    pre = pre + embed_one[None, :, None]
    first = jax.nn.silu(pre).astype(jnp.bfloat16)
    framed = jnp.pad(first, ((1, 1), (0, 0), (0, 0)))
    middle = jnp.zeros((FRAMES, HID, HEIGHT * WIDTH), jnp.float32)
    for lagged in range(3):
        middle = middle + jnp.einsum("oc,fcp->fop", temporal_weight[lagged].astype(jnp.float32), framed[lagged:lagged + FRAMES].astype(jnp.float32))
    second = jax.nn.silu(middle).astype(jnp.bfloat16)
    return jnp.einsum("ch,fhp->fcp", out_weight.astype(jnp.float32), second.astype(jnp.float32))


def reference(window_states, spatial_weight, temporal_weight, out_weight, time_embed, step_size, time_index, slides):
    states = window_states
    offset = jnp.zeros((), jnp.int32)
    for sweep in range(ITERS):
        indices = lax.dynamic_slice_in_dim(time_index, offset, WIN)
        embed = time_embed[indices]
        deltas = step_size[indices]
        drifts = lax.map(lambda item: drift_one(item, spatial_weight, temporal_weight, out_weight), (states, embed))
        weighted = deltas[:, None, None, None] * drifts
        running = jnp.cumsum(weighted, axis=0)
        updated = states[0][None] + (running - weighted)
        tail = states[0] + running[-1]
        extended = jnp.concatenate([updated, jnp.broadcast_to(tail[None], updated.shape)], axis=0)
        states = lax.dynamic_slice_in_dim(extended, slides[sweep].astype(jnp.int32), WIN)
        offset = offset + slides[sweep].astype(jnp.int32)
    return states
```

```python
import functools

import jax
import jax.numpy as jnp
from jax import lax
from jax.experimental import pallas as pl
from jax.experimental.pallas import tpu as pltpu
from jax.sharding import PartitionSpec as P

HEIGHT = 16
WIDTH = 32
ITERS = 2
CHUNK = 256
MESH = pl.DeviceIdType.MESH


def kernel(
    slabs,
    ranks,
    states_ref,
    spatial_ref,
    temporal_ref,
    out_weight_ref,
    embed_ref,
    step_ref,
    index_ref,
    slides_ref,
    result_ref,
    latent,
    first,
    held,
    wide_spatial,
    wide_temporal,
    column_embed,
    edges_0,
    inner_0,
    edges_1,
    inner_1,
    halo_send,
    halo_recv,
    sum_send,
    sum_recv,
):
    times, frames, channels, cells = states_ref.shape
    window = times * ranks
    hidden = spatial_ref.shape[0]
    rank = lax.axis_index("tm")
    slab = lax.axis_index("slab")
    has_left = slab > 0
    has_right = slab < slabs - 1
    edges = (edges_0, edges_1)
    inner = (inner_0, inner_1)

    barrier = pltpu.get_barrier_semaphore()

    @pl.when(has_left)
    def _():
        pl.semaphore_signal(barrier, inc=1, device_id={"slab": slab - 1}, device_id_type=MESH)

    @pl.when(has_right)
    def _():
        pl.semaphore_signal(barrier, inc=1, device_id={"slab": slab + 1}, device_id_type=MESH)

    for ahead in range(1, ranks):
        partner = lax.rem(rank + ahead, ranks)
        pl.semaphore_signal(barrier, inc=1, device_id={"tm": partner}, device_id_type=MESH)

    cell = lax.broadcasted_iota(jnp.int32, (channels, cells), 1)
    row, col = cell // WIDTH, cell % WIDTH
    keep = lambda flag: jnp.where(flag, 1.0, 0.0).astype(jnp.float32)
    has_west, has_east = keep(col > 0), keep(col < WIDTH - 1)
    has_north, has_south = keep(row > 0), keep(row < HEIGHT - 1)

    for frame in range(frames):
        for time in range(times):
            latent[0, frame + 1, time] = states_ref[time, frame].astype(jnp.bfloat16)

    def halo_copy(sweep, side):
        source, target, place = (1, frames + 1, slab - 1) if side == 0 else (frames, 0, slab + 1)
        return pltpu.make_async_remote_copy(
            src_ref=latent.at[sweep, source],
            dst_ref=latent.at[sweep, target],
            send_sem=halo_send.at[sweep, side],
            recv_sem=halo_recv.at[sweep, side],
            device_id={"slab": place},
            device_id_type=MESH,
        )

    def start_halo(sweep):
        @pl.when(has_left)
        def _():
            halo_copy(sweep, 0).start()

        @pl.when(has_right)
        def _():
            halo_copy(sweep, 1).start()

    def wait_halo(sweep):
        @pl.when(has_left)
        def _():
            halo_copy(sweep, 0).wait_send()
            halo_copy(sweep, 1).wait_recv()

        @pl.when(has_right)
        def _():
            halo_copy(sweep, 1).wait_send()
            halo_copy(sweep, 0).wait_recv()

    zero_frame = jnp.zeros((times, channels, cells), jnp.bfloat16)
    for sweep in range(ITERS):

        @pl.when(jnp.logical_not(has_left))
        def _():
            latent[sweep, 0] = zero_frame

        @pl.when(jnp.logical_not(has_right))
        def _():
            latent[sweep, frames + 1] = zero_frame

    greeted = has_left.astype(jnp.int32) + has_right.astype(jnp.int32) + (ranks - 1)
    pl.semaphore_wait(barrier, greeted)
    start_halo(0)

    half = jnp.asarray(0.5, jnp.bfloat16)
    wide_spatial[...] = spatial_ref[...] * half
    for lag in range(3):
        wide_temporal[:, lag * hidden : (lag + 1) * hidden] = temporal_ref[lag] * half

    def silu_half(h):
        return h + h * jnp.tanh(h)

    def first_of(sweep, place, valid):
        for time in range(times):
            x = latent[sweep, place, time].astype(jnp.float32)
            west = pltpu.roll(x, 1, 1) * has_west
            east = pltpu.roll(x, cells - 1, 1) * has_east
            mids = (west, x, east)
            above = [pltpu.roll(m, WIDTH, 1) * has_north for m in mids]
            below = [pltpu.roll(m, cells - WIDTH, 1) * has_south for m in mids]
            columns = jnp.concatenate(above + list(mids) + below, axis=0).astype(jnp.bfloat16)
            for at in range(0, cells, CHUNK):
                h = jnp.dot(
                    wide_spatial[...],
                    columns[:, at : at + CHUNK],
                    preferred_element_type=jnp.float32,
                )
                shift = column_embed[time]
                h = h + jnp.concatenate([shift] * (CHUNK // 128), axis=1)
                value = silu_half(h)
                if valid is not None:
                    value = value * valid
                first[time, place, :, at : at + CHUNK] = value.astype(jnp.bfloat16)

    def sums_of(steps, anchors, sums, frame, slot):
        for at in range(0, cells, CHUNK):
            lanes = slice(at, at + CHUNK)
            total = anchors(frame, lanes)
            for time in range(times):
                framed = first[time, pl.ds(frame, 3), :, lanes].reshape(3 * hidden, CHUNK)
                h = jnp.dot(wide_temporal[...], framed, preferred_element_type=jnp.float32)
                second = silu_half(h).astype(jnp.bfloat16)
                drift = jnp.dot(out_weight_ref[...], second, preferred_element_type=jnp.float32)
                total = total + steps[time] * drift
                sums[slot, rank * times + time, :, lanes] = total

    def sum_copy(sweep, sums, slot, frame, ahead, place):
        block = sums.at[slot, pl.ds(place * times, times)]
        return pltpu.make_async_remote_copy(
            src_ref=block,
            dst_ref=block,
            send_sem=sum_send.at[sweep, frame, ahead - 1],
            recv_sem=sum_recv.at[sweep, frame, ahead - 1],
            device_id={"tm": lax.rem(rank + ahead, ranks)},
            device_id_type=MESH,
        )

    def start_sums(sweep, sums, slot, frame):
        for ahead in range(1, ranks):
            sum_copy(sweep, sums, slot, frame, ahead, rank).start()

    def wait_sums(sweep, sums, slot, frame):
        for ahead in range(1, ranks):
            sum_copy(sweep, sums, slot, frame, ahead, rank).wait_send()
            source = lax.rem(rank + ranks - ahead, ranks)
            sum_copy(sweep, sums, slot, frame, ahead, source).wait_recv()

    def moved(sweep, sums, slot, time):
        place = slides_ref[sweep] + rank * times + time - 1
        place = jnp.clip(place, 0, window - 1)
        value = sums[slot, place]
        for lower in range(1, ranks):
            weight = jnp.where(place >= lower * times, 1.0, 0.0).astype(jnp.float32)
            value = value + weight * sums[slot, lower * times - 1]
        return value

    def new_states(sweep, sums, slot, frame):
        for time in range(times):
            value = moved(sweep, sums, slot, time)
            if sweep == ITERS - 1:
                result_ref[time, frame] = value
            else:
                if time == 0:
                    held[frame] = value
                latent[sweep + 1, frame + 1, time] = value.astype(jnp.bfloat16)

    edge_frames = (0, frames - 1)
    inner_frames = tuple(range(1, frames - 1))
    lead = jnp.where(rank == 0, 1.0, 0.0).astype(jnp.float32)
    offset = jnp.int32(0)
    for sweep in range(ITERS):
        steps = []
        for time in range(times):
            place = index_ref[offset + rank * times + time]
            steps.append(step_ref[place])
            line = embed_ref[pl.ds(place, 1), :] * 0.5
            column_embed[time] = jnp.transpose(jnp.broadcast_to(line, (128, hidden)))
        offset = offset + slides_ref[sweep]

        if sweep == 0:
            anchors = lambda frame, lanes: states_ref[0, frame, :, lanes] * lead
        else:
            anchors = lambda frame, lanes: held[frame, :, lanes] * lead

        @pl.loop(0, 2)
        def _(side):
            first_of(sweep, 1 + side * (frames - 1), None)

        if sweep > 0:
            for slot, frame in enumerate(inner_frames):
                wait_sums(sweep - 1, inner[sweep - 1], slot, frame)
            for slot, frame in enumerate(inner_frames):
                new_states(sweep - 1, inner[sweep - 1], slot, frame)

        @pl.loop(2, frames)
        def _(place):
            first_of(sweep, place, None)

        def edge_sums():
            wait_halo(sweep)

            @pl.loop(0, 2)
            def _(side):
                exists = jnp.where(side == 0, slab > 0, slab < slabs - 1)
                valid = jnp.where(exists, 1.0, 0.0).astype(jnp.float32)
                first_of(sweep, side * (frames + 1), valid)

            @pl.loop(0, 2)
            def _(side):
                frame = side * (frames - 1)
                sums_of(steps, anchors, edges[sweep], frame, side)
                start_sums(sweep, edges[sweep], side, frame)

        def inner_sums():
            @pl.loop(1, frames - 1)
            def _(frame):
                sums_of(steps, anchors, inner[sweep], frame, frame - 1)
                start_sums(sweep, inner[sweep], frame - 1, frame)

        def edge_states():
            for slot, frame in enumerate(edge_frames):
                wait_sums(sweep, edges[sweep], slot, frame)
            for slot, frame in enumerate(edge_frames):
                new_states(sweep, edges[sweep], slot, frame)

        if sweep < ITERS - 1:
            edge_sums()
            inner_sums()
            edge_states()
            start_halo(sweep + 1)
        else:
            inner_sums()
            edge_sums()
            for slot, frame in enumerate(inner_frames):
                wait_sums(sweep, inner[sweep], slot, frame)
            for slot, frame in enumerate(inner_frames):
                new_states(sweep, inner[sweep], slot, frame)
            edge_states()


def local(slabs, ranks, window_states, spatial_weight, temporal_weight, out_weight, time_embed, step_size, time_index, slides):
    times, frames, channels, cells = window_states.shape
    hidden = spatial_weight.shape[0]
    window = times * ranks
    f32, bf16 = jnp.float32, jnp.bfloat16
    vmem = pl.BlockSpec(memory_space=pltpu.VMEM)
    smem = pl.BlockSpec(memory_space=pltpu.SMEM)
    return pl.pallas_call(
        functools.partial(kernel, slabs, ranks),
        out_shape=jax.ShapeDtypeStruct(window_states.shape, f32),
        in_specs=[vmem] * 5 + [smem] * 3,
        out_specs=vmem,
        scratch_shapes=[
            pltpu.VMEM((ITERS, frames + 2, times, channels, cells), bf16),
            pltpu.VMEM((times, frames + 2, hidden, cells), bf16),
            pltpu.VMEM((frames, channels, cells), f32),
            pltpu.VMEM(spatial_weight.shape, bf16),
            pltpu.VMEM((hidden, 3 * hidden), bf16),
            pltpu.VMEM((times, hidden, 128), f32),
            pltpu.VMEM((2, window, channels, cells), f32),
            pltpu.VMEM((frames - 2, window, channels, cells), f32),
            pltpu.VMEM((2, window, channels, cells), f32),
            pltpu.VMEM((frames - 2, window, channels, cells), f32),
            pltpu.SemaphoreType.DMA((ITERS, 2)),
            pltpu.SemaphoreType.DMA((ITERS, 2)),
            pltpu.SemaphoreType.DMA((ITERS, frames, ranks - 1)),
            pltpu.SemaphoreType.DMA((ITERS, frames, ranks - 1)),
        ],
        compiler_params=pltpu.CompilerParams(
            collective_id=0, has_side_effects=True, vmem_limit_bytes=48 * 1024 * 1024
        ),
    )(window_states, spatial_weight, temporal_weight, out_weight, time_embed, step_size, time_index, slides)


def solution(mesh):
    return jax.shard_map(
        functools.partial(local, mesh.shape["slab"], mesh.shape["tm"]),
        mesh=mesh,
        in_specs=(
            P("tm", ("groups", "slab"), None, None),
            P(),
            P(),
            P(),
            P(),
            P(),
            P("groups"),
            P("groups"),
        ),
        out_specs=P("tm", ("groups", "slab"), None, None),
        check_vma=False,
    )
```

```python
import functools

import jax
import jax.numpy as jnp
from jax import lax
from jax.experimental import pallas as pl
from jax.experimental.pallas import tpu as pltpu
from jax.sharding import PartitionSpec as P

HEIGHT = 16
WIDTH = 32
ITERS = 2
CHUNK = 512
MESH = pl.DeviceIdType.MESH


def kernel(
    slabs,
    ranks,
    states_ref,
    spatial_ref,
    temporal_ref,
    out_weight_ref,
    embed_ref,
    step_ref,
    index_ref,
    slides_ref,
    result_ref,
    latent,
    first,
    held,
    wide_spatial,
    wide_temporal,
    column_embed,
    edges_0,
    inner_0,
    edges_1,
    inner_1,
    halo_send,
    halo_recv,
    sum_send,
    sum_recv,
):
    times, frames, channels, cells = states_ref.shape
    window = times * ranks
    hidden = spatial_ref.shape[1]
    rank = lax.axis_index("tm")
    slab = lax.axis_index("slab")
    has_left = slab > 0
    has_right = slab < slabs - 1
    edges = (edges_0, edges_1)
    inner = (inner_0, inner_1)

    barrier = pltpu.get_barrier_semaphore()

    @pl.when(has_left)
    def _():
        pl.semaphore_signal(barrier, inc=1, device_id={"slab": slab - 1}, device_id_type=MESH)

    @pl.when(has_right)
    def _():
        pl.semaphore_signal(barrier, inc=1, device_id={"slab": slab + 1}, device_id_type=MESH)

    for ahead in range(1, ranks):
        partner = lax.rem(rank + ahead, ranks)
        pl.semaphore_signal(barrier, inc=1, device_id={"tm": partner}, device_id_type=MESH)

    cell = lax.broadcasted_iota(jnp.int32, (channels, cells), 1)
    row, col = cell // WIDTH, cell % WIDTH
    keep = lambda flag: jnp.where(flag, 1.0, 0.0).astype(jnp.float32)
    has_west, has_east = keep(col > 0), keep(col < WIDTH - 1)
    has_north, has_south = keep(row > 0), keep(row < HEIGHT - 1)

    for frame in range(frames):
        for time in range(times):
            latent[0, frame + 1, time] = states_ref[time, frame].astype(jnp.bfloat16)

    def halo_copy(sweep, side):
        source, target, place = (1, frames + 1, slab - 1) if side == 0 else (frames, 0, slab + 1)
        return pltpu.make_async_remote_copy(
            src_ref=latent.at[sweep, source],
            dst_ref=latent.at[sweep, target],
            send_sem=halo_send.at[sweep, side],
            recv_sem=halo_recv.at[sweep, side],
            device_id={"slab": place},
            device_id_type=MESH,
        )

    def start_halo(sweep):
        @pl.when(has_left)
        def _():
            halo_copy(sweep, 0).start()

        @pl.when(has_right)
        def _():
            halo_copy(sweep, 1).start()

    def wait_halo(sweep):
        @pl.when(has_left)
        def _():
            halo_copy(sweep, 0).wait_send()
            halo_copy(sweep, 1).wait_recv()

        @pl.when(has_right)
        def _():
            halo_copy(sweep, 1).wait_send()
            halo_copy(sweep, 0).wait_recv()

    zero_frame = jnp.zeros((times, channels, cells), jnp.bfloat16)
    for sweep in range(ITERS):

        @pl.when(jnp.logical_not(has_left))
        def _():
            latent[sweep, 0] = zero_frame

        @pl.when(jnp.logical_not(has_right))
        def _():
            latent[sweep, frames + 1] = zero_frame

    greeted = has_left.astype(jnp.int32) + has_right.astype(jnp.int32) + (ranks - 1)
    pl.semaphore_wait(barrier, greeted)
    start_halo(0)

    half = jnp.asarray(0.5, jnp.bfloat16)
    turned = jnp.transpose(spatial_ref[...].astype(jnp.float32))
    wide_spatial[...] = (turned * 0.5).astype(jnp.bfloat16)
    for lag in range(3):
        wide_temporal[:, lag * hidden : (lag + 1) * hidden] = temporal_ref[lag] * half

    def embed_column(place):
        steps = embed_ref.shape[1]
        lane = lax.broadcasted_iota(jnp.int32, (hidden, 128), 1)
        picked = jnp.zeros((hidden, 128), jnp.float32)
        full = steps // 128 * 128
        for at in range(0, full, 128):
            picked = jnp.where(lane == place - at, embed_ref[:, at : at + 128], picked)
        column = jnp.sum(picked, axis=1, keepdims=True)
        if steps > full:
            block = embed_ref[:, full:]
            lane = lax.broadcasted_iota(jnp.int32, block.shape, 1)
            picked = jnp.where(lane == place - full, block, 0.0)
            column = column + jnp.sum(picked, axis=1, keepdims=True)
        return column

    def silu_half(h):
        return h + h * jnp.tanh(h)

    def first_of(sweep, place, valid):
        for time in range(times):
            x = latent[sweep, place, time].astype(jnp.float32)
            west = pltpu.roll(x, 1, 1) * has_west
            east = pltpu.roll(x, cells - 1, 1) * has_east
            mids = (west, x, east)
            above = [pltpu.roll(m, WIDTH, 1) * has_north for m in mids]
            below = [pltpu.roll(m, cells - WIDTH, 1) * has_south for m in mids]
            columns = jnp.concatenate(above + list(mids) + below, axis=0).astype(jnp.bfloat16)
            for at in range(0, cells, CHUNK):
                h = jnp.dot(
                    wide_spatial[...],
                    columns[:, at : at + CHUNK],
                    preferred_element_type=jnp.float32,
                )
                shift = column_embed[time]
                h = h + jnp.concatenate([shift] * (CHUNK // 128), axis=1)
                value = silu_half(h)
                if valid is not None:
                    value = value * valid
                first[time, place, :, at : at + CHUNK] = value.astype(jnp.bfloat16)

    def sums_of(steps, anchors, sums, frame, slot):
        for at in range(0, cells, CHUNK):
            lanes = slice(at, at + CHUNK)
            total = anchors(frame, lanes)
            for time in range(times):
                framed = first[time, pl.ds(frame, 3), :, lanes].reshape(3 * hidden, CHUNK)
                h = jnp.dot(wide_temporal[...], framed, preferred_element_type=jnp.float32)
                second = silu_half(h).astype(jnp.bfloat16)
                drift = jnp.dot(out_weight_ref[...], second, preferred_element_type=jnp.float32)
                total = total + steps[time] * drift
                sums[slot, rank * times + time, :, lanes] = total

    def sum_copy(sweep, sums, slot, frame, ahead, place):
        block = sums.at[slot, pl.ds(place * times, times)]
        return pltpu.make_async_remote_copy(
            src_ref=block,
            dst_ref=block,
            send_sem=sum_send.at[sweep, frame, ahead - 1],
            recv_sem=sum_recv.at[sweep, frame, ahead - 1],
            device_id={"tm": lax.rem(rank + ahead, ranks)},
            device_id_type=MESH,
        )

    def start_sums(sweep, sums, slot, frame):
        for ahead in range(1, ranks):
            sum_copy(sweep, sums, slot, frame, ahead, rank).start()

    def wait_sums(sweep, sums, slot, frame):
        for ahead in range(1, ranks):
            sum_copy(sweep, sums, slot, frame, ahead, rank).wait_send()
            source = lax.rem(rank + ranks - ahead, ranks)
            sum_copy(sweep, sums, slot, frame, ahead, source).wait_recv()

    def moved(sweep, sums, slot, time):
        place = slides_ref[sweep] + rank * times + time - 1
        place = jnp.clip(place, 0, window - 1)
        value = sums[slot, place]
        for lower in range(1, ranks):
            weight = jnp.where(place >= lower * times, 1.0, 0.0).astype(jnp.float32)
            value = value + weight * sums[slot, lower * times - 1]
        return value

    def new_states(sweep, sums, slot, frame):
        for time in range(times):
            value = moved(sweep, sums, slot, time)
            if sweep == ITERS - 1:
                result_ref[time, frame] = value
            else:
                if time == 0:
                    held[frame] = value
                latent[sweep + 1, frame + 1, time] = value.astype(jnp.bfloat16)

    edge_frames = (0, frames - 1)
    inner_frames = tuple(range(1, frames - 1))
    lead = jnp.where(rank == 0, 1.0, 0.0).astype(jnp.float32)
    offset = jnp.int32(0)
    for sweep in range(ITERS):
        steps = []
        for time in range(times):
            place = index_ref[offset + rank * times + time]
            steps.append(step_ref[place])
            column = embed_column(place) * 0.5
            column_embed[time] = jnp.broadcast_to(column, (hidden, 128))
        offset = offset + slides_ref[sweep]

        if sweep == 0:
            anchors = lambda frame, lanes: states_ref[0, frame, :, lanes] * lead
        else:
            anchors = lambda frame, lanes: held[frame, :, lanes] * lead

        @pl.loop(0, 2)
        def _(side):
            first_of(sweep, 1 + side * (frames - 1), None)

        if sweep > 0:
            for slot, frame in enumerate(inner_frames):
                wait_sums(sweep - 1, inner[sweep - 1], slot, frame)
            for slot, frame in enumerate(inner_frames):
                new_states(sweep - 1, inner[sweep - 1], slot, frame)

        @pl.loop(2, frames)
        def _(place):
            first_of(sweep, place, None)

        def edge_sums():
            wait_halo(sweep)

            @pl.loop(0, 2)
            def _(side):
                exists = jnp.where(side == 0, slab > 0, slab < slabs - 1)
                valid = jnp.where(exists, 1.0, 0.0).astype(jnp.float32)
                first_of(sweep, side * (frames + 1), valid)

            @pl.loop(0, 2)
            def _(side):
                frame = side * (frames - 1)
                sums_of(steps, anchors, edges[sweep], frame, side)
                start_sums(sweep, edges[sweep], side, frame)

        def inner_sums():
            @pl.loop(1, frames - 1)
            def _(frame):
                sums_of(steps, anchors, inner[sweep], frame, frame - 1)
                start_sums(sweep, inner[sweep], frame - 1, frame)

        def edge_states():
            for slot, frame in enumerate(edge_frames):
                wait_sums(sweep, edges[sweep], slot, frame)
            for slot, frame in enumerate(edge_frames):
                new_states(sweep, edges[sweep], slot, frame)

        if sweep < ITERS - 1:
            edge_sums()
            inner_sums()
            edge_states()
            start_halo(sweep + 1)
        else:
            inner_sums()
            edge_sums()
            for slot, frame in enumerate(inner_frames):
                wait_sums(sweep, inner[sweep], slot, frame)
            for slot, frame in enumerate(inner_frames):
                new_states(sweep, inner[sweep], slot, frame)
            edge_states()


def local(slabs, ranks, window_states, spatial_weight, temporal_weight, out_weight, time_embed, step_size, time_index, slides):
    times, frames, channels, cells = window_states.shape
    hidden = spatial_weight.shape[0]
    window = times * ranks
    f32, bf16 = jnp.float32, jnp.bfloat16
    vmem = pl.BlockSpec(memory_space=pltpu.VMEM)
    smem = pl.BlockSpec(memory_space=pltpu.SMEM)
    return pl.pallas_call(
        functools.partial(kernel, slabs, ranks),
        out_shape=jax.ShapeDtypeStruct(window_states.shape, f32),
        in_specs=[vmem] * 5 + [smem] * 3,
        out_specs=vmem,
        scratch_shapes=[
            pltpu.VMEM((ITERS, frames + 2, times, channels, cells), bf16),
            pltpu.VMEM((times, frames + 2, hidden, cells), bf16),
            pltpu.VMEM((frames, channels, cells), f32),
            pltpu.VMEM(spatial_weight.shape, bf16),
            pltpu.VMEM((hidden, 3 * hidden), bf16),
            pltpu.VMEM((times, hidden, 128), f32),
            pltpu.VMEM((2, window, channels, cells), f32),
            pltpu.VMEM((frames - 2, window, channels, cells), f32),
            pltpu.VMEM((2, window, channels, cells), f32),
            pltpu.VMEM((frames - 2, window, channels, cells), f32),
            pltpu.SemaphoreType.DMA((ITERS, 2)),
            pltpu.SemaphoreType.DMA((ITERS, 2)),
            pltpu.SemaphoreType.DMA((ITERS, frames, ranks - 1)),
            pltpu.SemaphoreType.DMA((ITERS, frames, ranks - 1)),
        ],
        compiler_params=pltpu.CompilerParams(
            collective_id=0, has_side_effects=True, vmem_limit_bytes=48 * 1024 * 1024
        ),
    )(window_states, spatial_weight.T, temporal_weight, out_weight, time_embed.T, step_size, time_index, slides)


def solution(mesh):
    return jax.shard_map(
        functools.partial(local, mesh.shape["slab"], mesh.shape["tm"]),
        mesh=mesh,
        in_specs=(
            P("tm", ("groups", "slab"), None, None),
            P(),
            P(),
            P(),
            P(),
            P(),
            P("groups"),
            P("groups"),
        ),
        out_specs=P("tm", ("groups", "slab"), None, None),
        check_vma=False,
    )
```

```python
import functools

import jax
import jax.numpy as jnp
from jax import lax
from jax.experimental import pallas as pl
from jax.experimental.pallas import tpu as pltpu
from jax.sharding import PartitionSpec as P

HEIGHT = 16
WIDTH = 32
ITERS = 2
UNIT = 256
MESH = pl.DeviceIdType.MESH


def kernel(
    slabs,
    ranks,
    states_ref,
    spatial_ref,
    temporal_ref,
    out_weight_ref,
    embed_ref,
    step_ref,
    index_ref,
    slides_ref,
    result_ref,
    latent,
    first,
    held,
    wide_spatial,
    wide_temporal,
    wide_out,
    column_embed,
    edges_0,
    inner_0,
    edges_1,
    inner_1,
    halo_send,
    halo_recv,
    sum_send,
    sum_recv,
):
    times, frames, channels, cells = states_ref.shape
    window = times * ranks
    hidden = spatial_ref.shape[1]
    rank = lax.axis_index("tm")
    slab = lax.axis_index("slab")
    has_left = slab > 0
    has_right = slab < slabs - 1
    edges = (edges_0, edges_1)
    inner = (inner_0, inner_1)

    barrier = pltpu.get_barrier_semaphore()

    @pl.when(has_left)
    def _():
        pl.semaphore_signal(barrier, inc=1, device_id={"slab": slab - 1}, device_id_type=MESH)

    @pl.when(has_right)
    def _():
        pl.semaphore_signal(barrier, inc=1, device_id={"slab": slab + 1}, device_id_type=MESH)

    for ahead in range(1, ranks):
        partner = lax.rem(rank + ahead, ranks)
        pl.semaphore_signal(barrier, inc=1, device_id={"tm": partner}, device_id_type=MESH)

    cell = lax.broadcasted_iota(jnp.int32, (channels, cells), 1)
    row, col = cell // WIDTH, cell % WIDTH
    keep = lambda flag: jnp.where(flag, 1.0, 0.0).astype(jnp.float32)
    has_west, has_east = keep(col > 0), keep(col < WIDTH - 1)
    has_north, has_south = keep(row > 0), keep(row < HEIGHT - 1)

    for frame in range(frames):
        for time in range(times):
            latent[0, frame + 1, time] = states_ref[time, frame].astype(jnp.bfloat16)

    def halo_copy(sweep, side):
        source, target, place = (1, frames + 1, slab - 1) if side == 0 else (frames, 0, slab + 1)
        return pltpu.make_async_remote_copy(
            src_ref=latent.at[sweep, source],
            dst_ref=latent.at[sweep, target],
            send_sem=halo_send.at[sweep, side],
            recv_sem=halo_recv.at[sweep, side],
            device_id={"slab": place},
            device_id_type=MESH,
        )

    def start_halo(sweep):
        @pl.when(has_left)
        def _():
            halo_copy(sweep, 0).start()

        @pl.when(has_right)
        def _():
            halo_copy(sweep, 1).start()

    def wait_halo(sweep):
        @pl.when(has_left)
        def _():
            halo_copy(sweep, 0).wait_send()
            halo_copy(sweep, 1).wait_recv()

        @pl.when(has_right)
        def _():
            halo_copy(sweep, 1).wait_send()
            halo_copy(sweep, 0).wait_recv()

    zero_frame = jnp.zeros((times, channels, cells), jnp.bfloat16)
    for sweep in range(ITERS):

        @pl.when(jnp.logical_not(has_left))
        def _():
            latent[sweep, 0] = zero_frame

        @pl.when(jnp.logical_not(has_right))
        def _():
            latent[sweep, frames + 1] = zero_frame

    greeted = has_left.astype(jnp.int32) + has_right.astype(jnp.int32) + (ranks - 1)
    pl.semaphore_wait(barrier, greeted)
    start_halo(0)

    half = jnp.asarray(0.5, jnp.bfloat16)
    turned = jnp.transpose(spatial_ref[...].astype(jnp.float32))
    wide_spatial[...] = (turned * 0.5).astype(jnp.bfloat16)
    for lag in range(3):
        wide_temporal[:, lag * hidden : (lag + 1) * hidden] = temporal_ref[lag] * half

    minor = hidden % UNIT
    major = hidden - minor
    wide_out[...] = jnp.zeros_like(wide_out)
    for time in range(times):
        rows, lanes = slice(time * channels, (time + 1) * channels), slice(time * minor, (time + 1) * minor)
        wide_out[rows, lanes] = out_weight_ref[:, major:]

    def embed_column(place):
        steps = embed_ref.shape[1]
        lane = lax.broadcasted_iota(jnp.int32, (hidden, 128), 1)
        picked = jnp.zeros((hidden, 128), jnp.float32)
        full = steps // 128 * 128
        for at in range(0, full, 128):
            picked = jnp.where(lane == place - at, embed_ref[:, at : at + 128], picked)
        column = jnp.sum(picked, axis=1, keepdims=True)
        if steps > full:
            block = embed_ref[:, full:]
            lane = lax.broadcasted_iota(jnp.int32, block.shape, 1)
            picked = jnp.where(lane == place - full, block, 0.0)
            column = column + jnp.sum(picked, axis=1, keepdims=True)
        return column

    def silu_half(h):
        return h + h * jnp.tanh(h)

    def columns_of(sweep, place, time):
        x = latent[sweep, place, time].astype(jnp.float32)
        west = pltpu.roll(x, 1, 1) * has_west
        east = pltpu.roll(x, cells - 1, 1) * has_east
        mids = (west, x, east)
        above = [pltpu.roll(m, WIDTH, 1) * has_north for m in mids]
        below = [pltpu.roll(m, cells - WIDTH, 1) * has_south for m in mids]
        return jnp.concatenate(above + list(mids) + below, axis=0).astype(jnp.bfloat16)

    def first_of(sweep, places):
        def finish(place, time, valid, h):
            shift = column_embed[time]
            value = silu_half(h + jnp.concatenate([shift] * (cells // 128), axis=1))
            if valid is not None:
                value = value * valid
            first[time, place] = value.astype(jnp.bfloat16)

        behind = None
        for place, valid in places:
            for time in range(times):
                h = jnp.dot(
                    wide_spatial[...],
                    columns_of(sweep, place, time),
                    preferred_element_type=jnp.float32,
                )
                if behind is not None:
                    finish(*behind)
                behind = (place, time, valid, h)
        finish(*behind)

    def sums_of(steps, anchors, sums, places, done):
        def project(frame, slot, seconds):
            rests = jnp.concatenate([second[major:] for second in seconds], axis=0)
            rest = jnp.dot(wide_out[...], rests, preferred_element_type=jnp.float32)
            total = anchors(frame)
            for time, second in enumerate(seconds):
                drift = jnp.dot(
                    out_weight_ref[:, :major], second[:major], preferred_element_type=jnp.float32
                )
                drift = drift + rest[time * channels : (time + 1) * channels]
                total = total + steps[time] * drift
                sums[slot, rank * times + time] = total
            done(slot, frame)

        behind = None
        seconds = []

        def finish(frame, slot, h):
            seconds.append(silu_half(h).astype(jnp.bfloat16))
            if len(seconds) == times:
                project(frame, slot, list(seconds))
                seconds.clear()

        for slot, frame in enumerate(places):
            for time in range(times):
                framed = first[time, frame : frame + 3].reshape(3 * hidden, cells)
                h = jnp.dot(wide_temporal[...], framed, preferred_element_type=jnp.float32)
                if behind is not None:
                    finish(*behind)
                behind = (frame, slot, h)
        finish(*behind)

    def sum_copy(sweep, sums, slot, frame, ahead, place):
        block = sums.at[slot, pl.ds(place * times, times)]
        return pltpu.make_async_remote_copy(
            src_ref=block,
            dst_ref=block,
            send_sem=sum_send.at[sweep, frame, ahead - 1],
            recv_sem=sum_recv.at[sweep, frame, ahead - 1],
            device_id={"tm": lax.rem(rank + ahead, ranks)},
            device_id_type=MESH,
        )

    def start_sums(sweep, sums, slot, frame):
        for ahead in range(1, ranks):
            sum_copy(sweep, sums, slot, frame, ahead, rank).start()

    def wait_sums(sweep, sums, slot, frame):
        for ahead in range(1, ranks):
            sum_copy(sweep, sums, slot, frame, ahead, rank).wait_send()
            source = lax.rem(rank + ranks - ahead, ranks)
            sum_copy(sweep, sums, slot, frame, ahead, source).wait_recv()

    def moved(sweep, sums, slot, time):
        place = slides_ref[sweep] + rank * times + time - 1
        place = jnp.clip(place, 0, window - 1)
        value = sums[slot, place]
        for lower in range(1, ranks):
            weight = jnp.where(place >= lower * times, 1.0, 0.0).astype(jnp.float32)
            value = value + weight * sums[slot, lower * times - 1]
        return value

    def new_states(sweep, sums, slot, frame):
        for time in range(times):
            value = moved(sweep, sums, slot, time)
            if sweep == ITERS - 1:
                result_ref[time, frame] = value
            else:
                if time == 0:
                    held[frame] = value
                latent[sweep + 1, frame + 1, time] = value.astype(jnp.bfloat16)

    edge_frames = (0, frames - 1)
    inner_frames = tuple(range(1, frames - 1))
    lead = jnp.where(rank == 0, 1.0, 0.0).astype(jnp.float32)
    offset = jnp.int32(0)
    for sweep in range(ITERS):
        steps = []
        for time in range(times):
            place = index_ref[offset + rank * times + time]
            steps.append(step_ref[place])
            column = embed_column(place) * 0.5
            column_embed[time] = jnp.broadcast_to(column, (hidden, 128))
        offset = offset + slides_ref[sweep]

        if sweep == 0:
            anchors = lambda frame: states_ref[0, frame] * lead
        else:
            anchors = lambda frame: held[frame] * lead

        first_of(sweep, [(1, None), (frames, None)])

        if sweep > 0:
            for slot, frame in enumerate(inner_frames):
                wait_sums(sweep - 1, inner[sweep - 1], slot, frame)
            for slot, frame in enumerate(inner_frames):
                new_states(sweep - 1, inner[sweep - 1], slot, frame)

        first_of(sweep, [(frame + 1, None) for frame in inner_frames])

        def edge_sums():
            wait_halo(sweep)

            first_of(sweep, [(0, keep(has_left)), (frames + 1, keep(has_right))])
            done = lambda slot, frame: start_sums(sweep, edges[sweep], slot, frame)
            sums_of(steps, anchors, edges[sweep], edge_frames, done)

        def inner_sums():
            done = lambda slot, frame: start_sums(sweep, inner[sweep], slot, frame)
            sums_of(steps, anchors, inner[sweep], inner_frames, done)

        def edge_states():
            for slot, frame in enumerate(edge_frames):
                wait_sums(sweep, edges[sweep], slot, frame)
            for slot, frame in enumerate(edge_frames):
                new_states(sweep, edges[sweep], slot, frame)

        if sweep < ITERS - 1:
            edge_sums()
            inner_sums()
            edge_states()
            start_halo(sweep + 1)
        else:
            inner_sums()
            edge_sums()
            for slot, frame in enumerate(inner_frames):
                wait_sums(sweep, inner[sweep], slot, frame)
            for slot, frame in enumerate(inner_frames):
                new_states(sweep, inner[sweep], slot, frame)
            edge_states()


def local(slabs, ranks, window_states, spatial_weight, temporal_weight, out_weight, time_embed, step_size, time_index, slides):
    times, frames, channels, cells = window_states.shape
    hidden = spatial_weight.shape[0]
    window = times * ranks
    f32, bf16 = jnp.float32, jnp.bfloat16
    vmem = pl.BlockSpec(memory_space=pltpu.VMEM)
    smem = pl.BlockSpec(memory_space=pltpu.SMEM)
    return pl.pallas_call(
        functools.partial(kernel, slabs, ranks),
        out_shape=jax.ShapeDtypeStruct(window_states.shape, f32),
        in_specs=[vmem] * 5 + [smem] * 3,
        out_specs=vmem,
        scratch_shapes=[
            pltpu.VMEM((ITERS, frames + 2, times, channels, cells), bf16),
            pltpu.VMEM((times, frames + 2, hidden, cells), bf16),
            pltpu.VMEM((frames, channels, cells), f32),
            pltpu.VMEM(spatial_weight.shape, bf16),
            pltpu.VMEM((hidden, 3 * hidden), bf16),
            pltpu.VMEM((times * channels, times * (hidden % UNIT)), bf16),
            pltpu.VMEM((times, hidden, 128), f32),
            pltpu.VMEM((2, window, channels, cells), f32),
            pltpu.VMEM((frames - 2, window, channels, cells), f32),
            pltpu.VMEM((2, window, channels, cells), f32),
            pltpu.VMEM((frames - 2, window, channels, cells), f32),
            pltpu.SemaphoreType.DMA((ITERS, 2)),
            pltpu.SemaphoreType.DMA((ITERS, 2)),
            pltpu.SemaphoreType.DMA((ITERS, frames, ranks - 1)),
            pltpu.SemaphoreType.DMA((ITERS, frames, ranks - 1)),
        ],
        compiler_params=pltpu.CompilerParams(
            collective_id=0, has_side_effects=True, vmem_limit_bytes=48 * 1024 * 1024
        ),
    )(window_states, spatial_weight.T, temporal_weight, out_weight, time_embed.T, step_size, time_index, slides)


def solution(mesh):
    return jax.shard_map(
        functools.partial(local, mesh.shape["slab"], mesh.shape["tm"]),
        mesh=mesh,
        in_specs=(
            P("tm", ("groups", "slab"), None, None),
            P(),
            P(),
            P(),
            P(),
            P(),
            P("groups"),
            P("groups"),
        ),
        out_specs=P("tm", ("groups", "slab"), None, None),
        check_vma=False,
    )
```
